256 devices in a mesh: var: 64 (over y, z_lo, x), samp: 4 (over z_hi, core).
Axes of the slice: x: 4, y: 4, z: 8 (z_hi: 2, z_lo: 4; z = z_hi * 4 + z_lo), core: 2. Of those that a mesh axis runs over, the one named last changes fastest.
Arguments:
- dosages: bfloat16 [16384, 32768], P('samp', 'var'), as said below
- window_end: int32 [32768], P('var'), may hold values from 0 to 32767, as said below
Outputs:
- correlations: bfloat16 [32768, 2048], P('var')
The draws below stay inside these ranges and needn't reach their ends.
Inputs may be any that keep to these rules, and one draw needn't show every extreme that they name: For a variant in block b (of 512 variants), window_end lies in block b + 1, b + 2 or b + 3 (the same block reach for the whole block), clipped to 32767; some variant reaches the last variant of the block three ahead. `dosages`: dosages lie between 0 and 2.
All inputs are finite; a program needn't handle non-finite values.
Results may differ from the reference program's by a relative error of at most 0.0034.
Values may be sent and summed in bfloat16 or wider, within the bound.
No kernel may reach another device: no remote copies, remote signals or barrier semaphores. Data moves between devices by JAX's collectives and lax.ppermute only.
A program may use at most 64 MiB of HBM per device.

```python
import jax
import jax.numpy as jnp
from jax import lax

VB = 512
S_DEV = 4096
N_VAR = 64
N_SAMP = 4


def draw_dosages(key, part):
    total = S_DEV * N_SAMP
    count = VB * N_VAR
    key_freq, key_noise = jax.random.split(key, 2)
    freq = jnp.exp(jax.random.uniform(key_freq, (count,), jnp.float32, jnp.log(0.02), jnp.log(0.5)))
    ramp = 0.4 + 1.2 * jnp.arange(total, dtype=jnp.float32) / total
    noise = jax.random.normal(key_noise, (total, count), jnp.float32)
    base = 2.0 * freq[None, :] * ramp[:, None]
    values = base + 0.6 * jnp.sqrt(freq)[None, :] * noise
    return jnp.clip(values, 0.0, 2.0).astype(jnp.bfloat16)


def draw_window_end(key, part):
    count = VB * N_VAR
    key_reach, key_offset = jax.random.split(key)
    reach = jax.random.randint(key_reach, (N_VAR,), 1, 4, jnp.int32)
    reach = reach.at[0].set(3)
    offset = jax.random.randint(key_offset, (N_VAR, VB), 0, VB, jnp.int32)
    offset = offset.at[:, 0].set(VB - 1)
    block = jnp.arange(N_VAR, dtype=jnp.int32)
    ends = (block[:, None] + reach[:, None]) * VB + offset
    return jnp.minimum(ends, count - 1).reshape(count).astype(jnp.int32)


def setup_inputs(seed: int = 0) -> dict:
    key_of = jax.random.split(jax.random.key(seed), 3)
    return {
        "dosages": draw_dosages(jax.random.fold_in(key_of[2], 71), 0),
        "window_end": draw_window_end(jax.random.fold_in(key_of[2], 71), 0),
    }


def reference(dosages, window_end):
    total = dosages.shape[0]
    count = dosages.shape[1]
    data = dosages.astype(jnp.float32)
    mean = lax.optimization_barrier(jnp.sum(data, axis=0)) / total
    square = lax.optimization_barrier(jnp.sum(data * data, axis=0)) / total
    spread = 1.0 / jnp.sqrt(square - mean * mean + 1e-05)
    standard = ((data - mean[None, :]) * spread[None, :]).astype(jnp.bfloat16)
    padded = jnp.concatenate([standard, jnp.zeros((total, 3 * VB), jnp.bfloat16)], axis=1)
    columns = jnp.arange(4 * VB, dtype=jnp.int32)

    def one_block(block):
        start = (block * VB).astype(jnp.int32)
        own = lax.dynamic_slice_in_dim(padded, start, VB, 1)
        band = lax.dynamic_slice_in_dim(padded, start, 4 * VB, 1)
        gram = jnp.dot(own.T, band, preferred_element_type=jnp.float32)
        ends = lax.dynamic_slice_in_dim(window_end, start, VB, 0)
        target = start + columns
        keep = (columns[None, :] < VB) | (target[None, :] <= ends[:, None])
        return jnp.where(keep, gram / total, 0.0).astype(jnp.bfloat16)
    blocks = lax.map(one_block, jnp.arange(count // VB, dtype=jnp.int32))
    return blocks.reshape(count, 4 * VB)
```

```python
import functools

import jax
import jax.numpy as jnp
from jax import lax
from jax.experimental import pallas as pl
from jax.experimental.pallas import tpu as pltpu
from jax.sharding import PartitionSpec as P

AXES = ("var", "samp")
RING = 4
GROUPS = 4


def moved(value, pairs):
    return lax.ppermute(value, AXES, pairs)


def pairs_of(count, target):
    pairs = []
    for var in range(count):
        for samp in range(GROUPS):
            to = target(var, samp)
            if to is not None:
                pairs.append((var * GROUPS + samp, to[0] * GROUPS + to[1]))
    return pairs


def to_core(count):
    return pairs_of(count, lambda var, samp: (var, samp ^ 1))


def to_far(count):
    return pairs_of(count, lambda var, samp: (var, samp ^ 2))


def along_ring(count, step):
    return pairs_of(
        count, lambda var, samp: (var // RING * RING + (var + step) % RING, samp)
    )


def to_ring_before(count, offset=None):
    def target(var, samp):
        if var < RING:
            return None
        if offset is not None and (var + offset) % RING == RING - 1:
            return None
        return (var - RING, samp)

    return pairs_of(count, target)


def band_kernel(place, *refs):
    raw, (stats, out1, out2, out3, flat, turned) = refs[:8], refs[8:]
    x, core = place[0], place[1]
    row = pl.program_id(0)
    depth, width = raw[0].shape
    chunk = 256
    half = width // 2

    @pl.when(row == 0)
    def _():
        for index in range(8):
            mean = stats[index, 0:1, :]
            spread = stats[index, 1:2, :]
            for start in range(0, depth, chunk):
                piece = raw[index][start : start + chunk, :].astype(jnp.float32)
                piece = ((piece - mean) * spread).astype(jnp.bfloat16)
                flat[index, start : start + chunk, :] = piece
                if index < 4:
                    turned[index, :, start : start + chunk] = piece.T

    owner = lax.rem(x + row, RING)
    for step, out in ((1, out1), (2, out2), (3, out3)):
        other = lax.rem(row + step, RING)
        other = other + jnp.where(owner + step >= RING, RING, 0)
        for part in range(2):
            slot = jnp.where(core == part, 0, 1)
            out[slot, 0] = jnp.dot(
                turned[row, part * half : (part + 1) * half, :],
                flat[other],
                preferred_element_type=jnp.float32,
            )


def band_products(place, quarters, stats):
    depth, width = quarters[0].shape
    half = width // 2
    whole = pl.BlockSpec((depth, width), lambda row: (0, 0))
    out = jax.ShapeDtypeStruct((2, RING, half, width), jnp.float32)
    out_spec = pl.BlockSpec((2, 1, half, width), lambda row: (0, row, 0, 0))
    return pl.pallas_call(
        band_kernel,
        grid=(RING,),
        out_shape=[out] * 3,
        in_specs=[pl.BlockSpec(memory_space=pltpu.SMEM)]
        + [whole] * 8
        + [pl.BlockSpec((8, 2, width), lambda row: (0, 0, 0))],
        out_specs=[out_spec] * 3,
        scratch_shapes=[
            pltpu.VMEM((8, depth, width), jnp.bfloat16),
            pltpu.VMEM((4, width, depth), jnp.bfloat16),
        ],
        compiler_params=pltpu.CompilerParams(vmem_limit_bytes=56 * 1024 * 1024),
        cost_estimate=pl.CostEstimate(
            flops=24 * width * width * depth,
            bytes_accessed=16 * depth * width + 24 * width * width * 2,
            transcendentals=0,
        ),
    )(place, *quarters, stats)


def per_device(dosages, window_end):
    rows, width = dosages.shape
    count = lax.axis_size("var")
    total = rows * lax.axis_size("samp")
    var, samp = lax.axis_index("var"), lax.axis_index("samp")
    x, core = var % RING, samp % 2
    depth = rows // RING
    half = width // 2

    core_pairs, far_pairs = to_core(count), to_far(count)
    ring_pairs = {step: along_ring(count, step) for step in (1, 2, 3)}

    def quarter(step):
        return lax.dynamic_slice_in_dim(dosages, (x + step) % RING * depth, depth, 0)

    here = [quarter(0)] + [None] * 3
    ahead = [None] * 4
    ahead[0] = moved(here[0], to_ring_before(count, 0))
    for d in (1, 3, 2):
        here[d] = moved(quarter(RING - d), ring_pairs[RING - d])
    for d in (1, 3, 2):
        ahead[d] = moved(here[d], to_ring_before(count, d))

    data = dosages.astype(jnp.float32)
    sums = jnp.stack([jnp.sum(data, axis=0), jnp.sum(data * data, axis=0)])
    sums = sums + moved(sums, core_pairs)
    sums = sums + moved(sums, far_pairs)
    mean = sums[0] / total
    spread = 1.0 / jnp.sqrt(sums[1] / total - mean * mean + 1e-05)
    own_stats = jnp.stack([mean, spread])
    ring_stats = [own_stats] + [
        moved(own_stats, ring_pairs[RING - d]) for d in (1, 2, 3)
    ]
    ring_stats = jnp.stack(ring_stats)
    stats = jnp.concatenate([ring_stats, moved(ring_stats, to_ring_before(count))])

    standard = ((data - mean[None, :]) * spread[None, :]).astype(jnp.bfloat16)
    own = jnp.einsum("sa,sb->ab", standard, standard, preferred_element_type=jnp.float32)
    kept = lax.dynamic_slice_in_dim(own, core * half, half, 0)
    given = lax.dynamic_slice_in_dim(own, (1 - core) * half, half, 0)
    partial = [kept + moved(given, core_pairs)]

    place = jnp.stack([x, core]).astype(jnp.int32)
    for product in band_products(place, here + ahead, stats):
        product = product[0] + moved(product[1], core_pairs)
        parts = product[0]
        for d in (1, 3, 2):
            parts = parts + moved(product[d].astype(jnp.bfloat16), ring_pairs[d])
        partial.append(parts)

    ends = lax.dynamic_slice_in_dim(window_end, core * half, half, 0)
    columns = jnp.arange(width, dtype=jnp.int32)
    tiles = []
    for step, value in enumerate(partial):
        value = value.astype(jnp.bfloat16)
        other = moved(value, far_pairs)
        gram = value.astype(jnp.float32) + other.astype(jnp.float32)
        if step:
            target = (var + step) * width + columns
            gram = jnp.where(target[None, :] <= ends[:, None], gram, 0.0)
        mine = (gram / total).astype(jnp.bfloat16)
        theirs = moved(mine, core_pairs)
        first = jnp.where(core == 0, mine, theirs)
        second = jnp.where(core == 0, theirs, mine)
        tiles.append(jnp.concatenate([first, second], axis=0))
    return jnp.concatenate(tiles, axis=1)


def solution(mesh):
    placed = (P("samp", "var"), P("var"))
    return jax.shard_map(
        per_device, mesh=mesh, in_specs=placed, out_specs=P("var", None), check_vma=False
    )
```

```python
import jax
import jax.numpy as jnp
from jax import lax
from jax.experimental import pallas as pl
from jax.experimental.pallas import tpu as pltpu
from jax.sharding import PartitionSpec as P

AXES = ("var", "samp")
RING = 4
GROUPS = 4
EXTRA = 16


def moved(value, pairs):
    return lax.ppermute(value, AXES, pairs)


def pairs_of(count, target):
    pairs = []
    for var in range(count):
        for samp in range(GROUPS):
            to = target(var, samp)
            if to is not None:
                pairs.append((var * GROUPS + samp, to[0] * GROUPS + to[1]))
    return pairs


def to_core(count):
    return pairs_of(count, lambda var, samp: (var, samp ^ 1))


def to_far(count):
    return pairs_of(count, lambda var, samp: (var, samp ^ 2))


def along_ring(count, step):
    return pairs_of(
        count, lambda var, samp: (var // RING * RING + (var + step) % RING, samp)
    )


def to_ring_before(count, step=None):
    def target(var, samp):
        if var < RING or (step is not None and var % RING == RING - 1):
            return None
        return (var // RING * RING - RING + (var + (step or 0)) % RING, samp)

    return pairs_of(count, target)


ANYWHERE = pl.BlockSpec(memory_space=pl.ANY)
SCALARS = pl.BlockSpec(memory_space=pltpu.SMEM)
WHOLE = pl.BlockSpec(memory_space=pltpu.VMEM)


def settings(mebibytes=56):
    return pltpu.CompilerParams(vmem_limit_bytes=mebibytes * 1024 * 1024)


FREE = pl.CostEstimate(flops=0, bytes_accessed=0, transcendentals=0)


def quarters_of(place, dosages, stats):
    rows, width = dosages.shape
    depth = rows // RING

    def kernel(place, data, stats, *refs):
        outs, every, sems = refs[:RING], refs[RING], refs[-1]
        copies = []
        for index in range(RING):
            start = pl.multiple_of(lax.rem(place[0] + index, RING) * depth, depth)
            for source, out, sem in (
                (data.at[pl.ds(start, depth), :], outs[index], 0),
                (data.at[pl.ds(index * depth, depth), :], every.at[index], 1),
            ):
                target = out.at[pl.ds(0, depth), :]
                copies.append(pltpu.make_async_copy(source, target, sems.at[sem, index]))
        for copy in copies:
            copy.start()
        terms, rest = [], stats[...]
        for _ in range(3):
            term = rest.astype(jnp.bfloat16)
            terms.append(term.astype(jnp.float32))
            rest = rest - terms[-1]
        terms.append(jnp.zeros((EXTRA - 9, width), jnp.float32))
        terms = jnp.concatenate(terms, axis=0).astype(jnp.bfloat16)
        for index in range(RING):
            outs[index][depth:, :] = terms
            every[index, depth:, :] = terms
        for copy in copies:
            copy.wait()

    return pl.pallas_call(
        kernel,
        in_specs=[SCALARS, ANYWHERE, WHOLE],
        out_specs=[WHOLE] * (RING + 1),
        out_shape=[jax.ShapeDtypeStruct((depth + EXTRA, width), dosages.dtype)] * RING
        + [jax.ShapeDtypeStruct((RING, depth + EXTRA, width), dosages.dtype)],
        scratch_shapes=[pltpu.SemaphoreType.DMA((2, RING))],
        compiler_params=settings(),
        cost_estimate=FREE,
    )(place, dosages, stats)


def carried(rows):
    rows = rows.astype(jnp.float32)
    return (rows[0:3] + rows[3:6]) + rows[6:9]


def standardized(piece, stats):
    piece = piece.astype(jnp.float32)
    return ((piece - stats[0:1, :]) * stats[1:2, :]).astype(jnp.bfloat16)


def own_product(place, dosages, stats):
    rows, width = dosages.shape
    half, chunk = width // 2, 1024

    def kernel(place, data, stats, kept, given, total, turned):
        step = pl.program_id(0)
        flat = standardized(data[...], stats)
        for start in range(0, chunk, 256):
            turned[:, start : start + 256] = flat[start : start + 256, :].T
        product = jnp.dot(turned[...], flat, preferred_element_type=jnp.float32)

        @pl.when(step == 0)
        def _():
            total[...] = product

        @pl.when(step > 0)
        def _():
            total[...] += product

        @pl.when(step == pl.num_programs(0) - 1)
        def _():
            core = place[1]
            kept[...] = total[pl.ds(pl.multiple_of(core * half, half), half), :]
            other = total[pl.ds(pl.multiple_of((1 - core) * half, half), half), :]
            given[...] = other.astype(jnp.bfloat16)

    fixed = lambda i: (0, 0)
    return pl.pallas_call(
        kernel,
        grid=(rows // chunk,),
        in_specs=[
            SCALARS,
            pl.BlockSpec((chunk, width), lambda i: (i, 0)),
            pl.BlockSpec(stats.shape, fixed),
        ],
        out_specs=[pl.BlockSpec((half, width), fixed)] * 2,
        out_shape=[
            jax.ShapeDtypeStruct((half, width), jnp.float32),
            jax.ShapeDtypeStruct((half, width), jnp.bfloat16),
        ],
        scratch_shapes=[
            pltpu.VMEM((width, width), jnp.float32),
            pltpu.VMEM((width, chunk), jnp.bfloat16),
        ],
        compiler_params=settings(),
        cost_estimate=FREE,
    )(place, dosages, stats)


def prepared(place, quarters, after):
    count, depth, width = quarters.shape
    depth -= EXTRA
    half = width // 2

    def kernel(place, raw, *refs):
        out, kept, given, stats = refs[-4:]
        stats[0] = carried(raw[0, depth:, :])
        out[0] = standardized(raw[0, :depth, :], stats.at[0])
        core = place[1]
        kept[0] = out[0, :, pl.ds(pl.multiple_of(core * half, half), half)]
        given[0] = out[0, :, pl.ds(pl.multiple_of((1 - core) * half, half), half)]

    shapes = [(2 * count, depth, width)] + [(count, depth, half)] * 2
    whole = lambda *shape: pl.BlockSpec((1, *shape), lambda i: (i, 0, 0))
    return pl.pallas_call(
        kernel,
        grid=(count,),
        in_specs=[SCALARS, whole(depth + EXTRA, width)] + [ANYWHERE] * len(after),
        out_specs=[whole(*shape[1:]) for shape in shapes] + [whole(3, width)],
        out_shape=[jax.ShapeDtypeStruct(shape, jnp.bfloat16) for shape in shapes]
        + [jax.ShapeDtypeStruct((count, 3, width), jnp.float32)],
        compiler_params=settings(),
        cost_estimate=FREE,
    )(place, quarters, *after)


def prepared_ahead(place, quarters, blocks):
    depth, width = quarters[0].shape
    depth -= EXTRA

    def kernel(place, *refs):
        raw, (out, stats, held, sems) = refs[:RING], refs[-4:]
        item = pl.program_id(0)
        for index in range(RING):
            copy = pltpu.make_async_copy(raw[index], held.at[index], sems.at[index])
            pl.when(item == 0)(copy.start)
        for index in range(RING):
            copy = pltpu.make_async_copy(raw[index], held.at[index], sems.at[index])
            pl.when(item == index)(copy.wait)
        stats[0] = carried(held[item, depth:, :])
        out[0] = standardized(held[item, :depth, :], stats.at[0])

    block = lambda i, place: lax.rem(place[0] + i, RING)
    return pl.pallas_call(
        kernel,
        grid_spec=pltpu.PrefetchScalarGridSpec(
            num_scalar_prefetch=1,
            grid=(RING,),
            in_specs=[ANYWHERE] * (RING + 1),
            out_specs=[
                pl.BlockSpec((1, depth, width), lambda i, place: (RING + block(i, place), 0, 0)),
                pl.BlockSpec((1, 3, width), lambda i, place: (block(i, place), 0, 0)),
            ],
            scratch_shapes=[
                pltpu.VMEM((RING, depth + EXTRA, width), jnp.bfloat16),
                pltpu.SemaphoreType.DMA((RING,)),
            ],
        ),
        out_shape=[
            jax.ShapeDtypeStruct(blocks.shape, blocks.dtype),
            jax.ShapeDtypeStruct((RING, 3, width), jnp.float32),
        ],
        input_output_aliases={1 + RING: 0},
        compiler_params=settings(),
        cost_estimate=FREE,
    )(place, *quarters, blocks)


def summed(own, parts, shared, after):
    half, width = own.shape
    count = len(parts)

    def kernel(own, *refs):
        parts, shared, out = refs[:count], refs[count], refs[-1]
        total = own[...]
        for part in parts:
            total = total + part[...].astype(jnp.float32)
        out[...] = (total - shared[...]).astype(jnp.bfloat16)

    return pl.pallas_call(
        kernel,
        in_specs=[WHOLE] * (count + 2) + [ANYWHERE] * len(after),
        out_shape=jax.ShapeDtypeStruct((half, width), jnp.bfloat16),
        compiler_params=settings(8),
        cost_estimate=FREE,
    )(own, *parts, shared, *after)


def assembled(place, mine, theirs):
    half, width = mine[0].shape
    count = len(mine)

    def kernel(place, *refs):
        out = refs[-1]
        core = place[1]
        for index in range(count):
            columns = slice(index * width, (index + 1) * width)
            out[pl.ds(pl.multiple_of(core * half, half), half), columns] = refs[index][...]
            out[pl.ds(pl.multiple_of((1 - core) * half, half), half), columns] = refs[
                count + index
            ][...]

    return pl.pallas_call(
        kernel,
        in_specs=[SCALARS] + [WHOLE] * (2 * count),
        out_shape=jax.ShapeDtypeStruct((2 * half, count * width), jnp.bfloat16),
        compiler_params=settings(),
        cost_estimate=FREE,
    )(place, *mine, *theirs)


def per_device(dosages, window_end):
    rows, width = dosages.shape
    count = lax.axis_size("var")
    total = rows * lax.axis_size("samp")
    var, samp = lax.axis_index("var"), lax.axis_index("samp")
    x, core = var % RING, samp % 2
    half = width // 2
    place = jnp.stack([x, core]).astype(jnp.int32)

    core_pairs, far_pairs = to_core(count), to_far(count)
    rings = [list(range(first, first + RING)) for first in range(0, count, RING)]

    data = dosages.astype(jnp.float32)
    sums = jnp.stack([jnp.sum(data, axis=0), jnp.sum(data * data, axis=0)])
    sums = jnp.stack([sums, moved(sums, far_pairs)])
    sums, far_sums = sums + moved(sums, core_pairs)
    mean = (sums[0] + far_sums[0]) / total
    spread = 1.0 / jnp.sqrt((sums[1] + far_sums[1]) / total - mean * mean + 1e-05)
    tilt = (sums[0] - far_sums[0]) / total * spread * (total / 2) ** 0.5
    own_stats = jnp.stack([mean, spread, tilt])

    *quarters, every = quarters_of(place, dosages, own_stats)
    ahead = [
        moved(quarters[-d % RING], to_ring_before(count, -d % RING)) for d in range(RING)
    ]
    here = lax.all_to_all(every, "var", 0, 0, axis_index_groups=rings)

    own_kept, own_given = own_product(place, dosages, own_stats)
    own = own_kept + moved(own_given, core_pairs).astype(jnp.float32)
    rising = lax.dynamic_slice_in_dim(tilt, core * half, half, 0)[:, None]
    values = [(own - rising * tilt[None, :]).astype(jnp.bfloat16)]
    blocks, kept_rows, given_rows, ring_stats = prepared(place, here, values)
    blocks, ahead_stats = prepared_ahead(place, ahead, blocks)
    tilts = jnp.concatenate([ring_stats[:, 2], ahead_stats[:, 2]])

    ends = lax.dynamic_slice_in_dim(window_end, core * half, half, 0)
    columns = jnp.arange(width, dtype=jnp.int32)

    def shared(step):
        return rising * lax.dynamic_slice_in_dim(tilts, x + step, 1, 0)

    def finished(step, value, other):
        both = rising * tilt[None, :] if step == 0 else shared(step)
        gram = value.astype(jnp.float32) + other.astype(jnp.float32) + 2.0 * both
        if step:
            target = (var + step) * width + columns
            gram = jnp.where(target[None, :] <= ends[:, None], gram, 0.0)
        return (gram / total).astype(jnp.bfloat16)

    far = [moved(values[0], far_pairs)]
    mine = [finished(0, values[0], far[0])]
    theirs = [moved(mine[0], core_pairs)]
    for step in (1, 2, 3):
        product = lambda left: jnp.einsum(
            "zsa,zsb->zab",
            left,
            blocks[step : step + RING],
            preferred_element_type=jnp.float32,
        )
        received = moved(product(given_rows).astype(jnp.bfloat16), core_pairs)
        kept = product(kept_rows)

        def part(d):
            at = lambda array: lax.dynamic_index_in_dim(array, (x + d) % RING, 0, False)
            return at(kept) + at(received).astype(jnp.float32)

        parts = [
            moved(part(d).astype(jnp.bfloat16), along_ring(count, d)) for d in (1, 3, 2)
        ]
        after = theirs[step - 2 : step - 1] if step > 1 else []
        values.append(summed(part(0), parts, shared(step), after))
        far.append(moved(values[step], far_pairs))
        mine.append(finished(step, values[step], far[step]))
        theirs.append(moved(mine[step], core_pairs))
    return assembled(place, mine, theirs)


def solution(mesh):
    placed = (P("samp", "var"), P("var"))
    return jax.shard_map(
        per_device, mesh=mesh, in_specs=placed, out_specs=P("var", None), check_vma=False
    )
```

```python
import jax
import jax.numpy as jnp
from jax import lax
from jax.experimental import pallas as pl
from jax.experimental.pallas import tpu as pltpu
from jax.sharding import PartitionSpec as P

AXES = ("var", "samp")
RING = 4
GROUPS = 4
EXTRA = 16


def moved(value, pairs):
    return lax.ppermute(value, AXES, pairs)


def pairs_of(count, target):
    pairs = []
    for var in range(count):
        for samp in range(GROUPS):
            to = target(var, samp)
            if to is not None:
                pairs.append((var * GROUPS + samp, to[0] * GROUPS + to[1]))
    return pairs


def to_core(count):
    return pairs_of(count, lambda var, samp: (var, samp ^ 1))


def to_far(count):
    return pairs_of(count, lambda var, samp: (var, samp ^ 2))


def along_ring(count, step):
    return pairs_of(
        count, lambda var, samp: (var // RING * RING + (var + step) % RING, samp)
    )


def to_ring_before(count):
    return pairs_of(count, lambda var, samp: None if var < RING else (var - RING, samp))


ANYWHERE = pl.BlockSpec(memory_space=pl.ANY)
SCALARS = pl.BlockSpec(memory_space=pltpu.SMEM)
WHOLE = pl.BlockSpec(memory_space=pltpu.VMEM)


def settings(mebibytes=56):
    return pltpu.CompilerParams(vmem_limit_bytes=mebibytes * 1024 * 1024)


FREE = pl.CostEstimate(flops=0, bytes_accessed=0, transcendentals=0)


def with_statistics(quarters, stats):
    count, depth, width = quarters.shape
    half = depth // 2

    def kernel(data, stats, out):
        out[0, :half, :] = data[0]
        terms, rest = [], stats[...]
        for _ in range(3):
            terms.append(rest.astype(jnp.bfloat16).astype(jnp.float32))
            rest = rest - terms[-1]
        terms.append(jnp.zeros((EXTRA - 9, width), jnp.float32))
        out[0, half:, :] = jnp.concatenate(terms, axis=0).astype(jnp.bfloat16)

    return pl.pallas_call(
        kernel,
        grid=(count,),
        in_specs=[
            pl.BlockSpec((1, half, width), lambda i: (i, 1, 0)),
            pl.BlockSpec(stats.shape, lambda i: (0, 0)),
        ],
        out_specs=pl.BlockSpec((1, half + EXTRA, width), lambda i: (i, 0, 0)),
        out_shape=jax.ShapeDtypeStruct((count, half + EXTRA, width), quarters.dtype),
        compiler_params=settings(8),
        cost_estimate=FREE,
    )(quarters, stats)


def behind(value, *others):
    def kernel(*refs):
        pass

    return pl.pallas_call(
        kernel,
        in_specs=[ANYWHERE] * (1 + len(others)),
        out_specs=ANYWHERE,
        out_shape=jax.ShapeDtypeStruct(value.shape, value.dtype),
        input_output_aliases={0: 0},
        compiler_params=settings(1),
        cost_estimate=FREE,
    )(value, *others)


def carried(rows):
    rows = rows.astype(jnp.float32)
    return (rows[0:3] + rows[3:6]) + rows[6:9]


def standardized(piece, stats):
    piece = piece.astype(jnp.float32)
    return ((piece - stats[0:1, :]) * stats[1:2, :]).astype(jnp.bfloat16)


def own_product(place, dosages, stats):
    rows, width = dosages.shape
    half, chunk = width // 2, 1024

    def kernel(place, data, stats, kept, given, total, turned):
        step = pl.program_id(0)
        flat = standardized(data[...], stats)
        for start in range(0, chunk, 256):
            turned[:, start : start + 256] = flat[start : start + 256, :].T
        product = jnp.dot(turned[...], flat, preferred_element_type=jnp.float32)

        @pl.when(step == 0)
        def _():
            total[...] = product

        @pl.when(step > 0)
        def _():
            total[...] += product

        @pl.when(step == pl.num_programs(0) - 1)
        def _():
            core = place[1]
            kept[...] = total[pl.ds(pl.multiple_of(core * half, half), half), :]
            other = total[pl.ds(pl.multiple_of((1 - core) * half, half), half), :]
            given[...] = other.astype(jnp.bfloat16)

    fixed = lambda i: (0, 0)
    return pl.pallas_call(
        kernel,
        grid=(rows // chunk,),
        in_specs=[
            SCALARS,
            pl.BlockSpec((chunk, width), lambda i: (i, 0)),
            pl.BlockSpec(stats.shape, fixed),
        ],
        out_specs=[pl.BlockSpec((half, width), fixed)] * 2,
        out_shape=[
            jax.ShapeDtypeStruct((half, width), jnp.float32),
            jax.ShapeDtypeStruct((half, width), jnp.bfloat16),
        ],
        scratch_shapes=[
            pltpu.VMEM((width, width), jnp.float32),
            pltpu.VMEM((width, chunk), jnp.bfloat16),
        ],
        compiler_params=settings(20),
        cost_estimate=FREE,
    )(place, dosages, stats)


def prepared(place, first, second, after):
    count, depth, width = first.shape
    half = width // 2

    def kernel(place, first, second, *refs):
        out, kept, given, stats = refs[-4:]
        stats[0] = carried(second[0, depth:, :])
        out[0, :depth, :] = standardized(first[0], stats.at[0])
        out[0, depth:, :] = standardized(second[0, :depth, :], stats.at[0])
        core = place[1]
        kept[0] = out[0, :, pl.ds(pl.multiple_of(core * half, half), half)]
        given[0] = out[0, :, pl.ds(pl.multiple_of((1 - core) * half, half), half)]

    shapes = [(2 * count - 1, 2 * depth, width)] + [(count, 2 * depth, half)] * 2
    whole = lambda *shape: pl.BlockSpec((1, *shape), lambda i: (i, 0, 0))
    return pl.pallas_call(
        kernel,
        grid=(count,),
        in_specs=[SCALARS, whole(depth, width), whole(depth + EXTRA, width)]
        + [ANYWHERE] * len(after),
        out_specs=[whole(*shape[1:]) for shape in shapes] + [whole(3, width)],
        out_shape=[jax.ShapeDtypeStruct(shape, jnp.bfloat16) for shape in shapes]
        + [jax.ShapeDtypeStruct((count, 3, width), jnp.float32)],
        compiler_params=settings(20),
        cost_estimate=FREE,
    )(place, first, second, *after)


def prepared_ahead(first, second, blocks):
    count, depth, width = first.shape

    def kernel(first, second, blocks, out, stats):
        stats[0] = carried(second[0, depth:, :])
        out[0, :depth, :] = standardized(first[0], stats.at[0])
        out[0, depth:, :] = standardized(second[0, :depth, :], stats.at[0])

    whole = lambda *shape: pl.BlockSpec((1, *shape), lambda i: (i, 0, 0))
    return pl.pallas_call(
        kernel,
        grid=(count,),
        in_specs=[whole(depth, width), whole(depth + EXTRA, width), ANYWHERE],
        out_specs=[
            pl.BlockSpec((1, 2 * depth, width), lambda i: (RING + i, 0, 0)),
            whole(3, width),
        ],
        out_shape=[
            jax.ShapeDtypeStruct(blocks.shape, blocks.dtype),
            jax.ShapeDtypeStruct((count, 3, width), jnp.float32),
        ],
        input_output_aliases={2: 0},
        compiler_params=settings(20),
        cost_estimate=FREE,
    )(first, second, blocks)


def summed(own, parts, shared, after):
    half, width = own.shape
    count = len(parts)

    def kernel(own, *refs):
        parts, shared, out = refs[:count], refs[count], refs[-1]
        total = own[...]
        for part in parts:
            total = total + part[...].astype(jnp.float32)
        out[...] = (total - shared[...]).astype(jnp.bfloat16)

    return pl.pallas_call(
        kernel,
        in_specs=[WHOLE] * (count + 2) + [ANYWHERE] * len(after),
        out_shape=jax.ShapeDtypeStruct((half, width), jnp.bfloat16),
        compiler_params=settings(8),
        cost_estimate=FREE,
    )(own, *parts, shared, *after)


def assembled(place, mine, theirs):
    half, width = mine[0].shape
    count = len(mine)

    def kernel(place, *refs):
        out = refs[-1]
        core = place[1]
        for index in range(count):
            columns = slice(index * width, (index + 1) * width)
            out[pl.ds(pl.multiple_of(core * half, half), half), columns] = refs[index][...]
            out[pl.ds(pl.multiple_of((1 - core) * half, half), half), columns] = refs[
                count + index
            ][...]

    return pl.pallas_call(
        kernel,
        in_specs=[SCALARS] + [WHOLE] * (2 * count),
        out_shape=jax.ShapeDtypeStruct((2 * half, count * width), jnp.bfloat16),
        compiler_params=settings(8),
        cost_estimate=FREE,
    )(place, *mine, *theirs)


def per_device(dosages, window_end):
    rows, width = dosages.shape
    count = lax.axis_size("var")
    total = rows * lax.axis_size("samp")
    var, samp = lax.axis_index("var"), lax.axis_index("samp")
    x, core = var % RING, samp % 2
    half = width // 2
    place = jnp.stack([x, core]).astype(jnp.int32)

    core_pairs, far_pairs = to_core(count), to_far(count)
    rings = [list(range(first, first + RING)) for first in range(0, count, RING)]

    data = dosages.astype(jnp.float32)
    sums = jnp.stack([jnp.sum(data, axis=0), jnp.sum(data * data, axis=0)])
    sums = jnp.stack([sums, moved(sums, far_pairs)])
    sums, far_sums = sums + moved(sums, core_pairs)
    mean = (sums[0] + far_sums[0]) / total
    spread = 1.0 / jnp.sqrt((sums[1] + far_sums[1]) / total - mean * mean + 1e-05)
    tilt = (sums[0] - far_sums[0]) / total * spread * (total / 2) ** 0.5
    own_stats = jnp.stack([mean, spread, tilt])

    all_quarters = dosages.reshape(RING, rows // RING, width)

    def dealt(value):
        return lax.all_to_all(value, "var", 0, 0, axis_index_groups=rings)

    here = [dealt(all_quarters[:, : rows // RING // 2])]
    here.append(dealt(behind(with_statistics(all_quarters, own_stats), here[0])))
    back_pairs = to_ring_before(count)
    ahead = [moved(here[0][: RING - 1], back_pairs)]
    ahead.append(moved(behind(here[1][: RING - 1], ahead[0]), back_pairs))

    own_kept, own_given = own_product(place, dosages, own_stats)
    own = own_kept + moved(own_given, core_pairs).astype(jnp.float32)
    rising = lax.dynamic_slice_in_dim(tilt, core * half, half, 0)[:, None]
    values = [(own - rising * tilt[None, :]).astype(jnp.bfloat16)]
    blocks, kept_rows, given_rows, ring_stats = prepared(place, *here, values + ahead[:1])
    blocks, ahead_stats = prepared_ahead(*ahead, blocks)
    tilts = jnp.concatenate([ring_stats[:, 2], ahead_stats[:, 2]])

    ends = lax.dynamic_slice_in_dim(window_end, core * half, half, 0)
    columns = jnp.arange(width, dtype=jnp.int32)

    def shared(step):
        return rising * lax.dynamic_slice_in_dim(tilts, x + step, 1, 0)

    def finished(step, value, other):
        both = rising * tilt[None, :] if step == 0 else shared(step)
        gram = value.astype(jnp.float32) + other.astype(jnp.float32) + 2.0 * both
        if step:
            target = (var + step) * width + columns
            gram = jnp.where(target[None, :] <= ends[:, None], gram, 0.0)
        return (gram / total).astype(jnp.bfloat16)

    far = [moved(behind(values[0], ahead[1]), far_pairs)]
    mine = [finished(0, values[0], far[0])]
    theirs = [moved(mine[0], core_pairs)]
    for step in (1, 2, 3):
        if step > 1:
            given_rows = behind(given_rows, received)
        product = lambda left: jnp.einsum(
            "zsa,zsb->zab",
            left,
            blocks[step : step + RING],
            preferred_element_type=jnp.float32,
        )
        received = moved(product(given_rows).astype(jnp.bfloat16), core_pairs)
        kept = product(kept_rows)

        def part(d):
            at = lambda array: lax.dynamic_index_in_dim(array, (x + d) % RING, 0, False)
            return at(kept) + at(received).astype(jnp.float32)

        parts = [
            moved(part(d).astype(jnp.bfloat16), along_ring(count, d)) for d in (1, 3, 2)
        ]
        after = theirs[step - 2 : step - 1] if step > 1 else []
        values.append(summed(part(0), parts, shared(step), after))
        far.append(moved(values[step], far_pairs))
        mine.append(finished(step, values[step], far[step]))
        theirs.append(moved(mine[step], core_pairs))
    return assembled(place, mine, theirs)


def solution(mesh):
    placed = (P("samp", "var"), P("var"))
    return jax.shard_map(
        per_device, mesh=mesh, in_specs=placed, out_specs=P("var", None), check_vma=False
    )
```

```python
import jax
import jax.numpy as jnp
from jax import lax
from jax.experimental import pallas as pl
from jax.experimental.pallas import tpu as pltpu
from jax.sharding import PartitionSpec as P

AXES = ("var", "samp")
RING = 4
GROUPS = 4
EXTRA = 16


def moved(value, pairs):
    return lax.ppermute(value, AXES, pairs)


def pairs_of(count, target):
    pairs = []
    for var in range(count):
        for samp in range(GROUPS):
            to = target(var, samp)
            if to is not None:
                pairs.append((var * GROUPS + samp, to[0] * GROUPS + to[1]))
    return pairs


def to_core(count):
    return pairs_of(count, lambda var, samp: (var, samp ^ 1))


def to_far(count):
    return pairs_of(count, lambda var, samp: (var, samp ^ 2))


def along_ring(count, step):
    return pairs_of(
        count, lambda var, samp: (var // RING * RING + (var + step) % RING, samp)
    )


def to_ring_before(count):
    return pairs_of(count, lambda var, samp: None if var < RING else (var - RING, samp))


ANYWHERE = pl.BlockSpec(memory_space=pl.ANY)
SCALARS = pl.BlockSpec(memory_space=pltpu.SMEM)
WHOLE = pl.BlockSpec(memory_space=pltpu.VMEM)


def settings(mebibytes=56):
    return pltpu.CompilerParams(vmem_limit_bytes=mebibytes * 1024 * 1024)


FREE = pl.CostEstimate(flops=0, bytes_accessed=0, transcendentals=0)


def with_statistics(quarters, stats):
    count, depth, width = quarters.shape
    half = depth // 2

    def kernel(data, stats, out):
        out[0, :half, :] = data[0]
        terms, rest = [], stats[...]
        for _ in range(3):
            terms.append(rest.astype(jnp.bfloat16).astype(jnp.float32))
            rest = rest - terms[-1]
        terms.append(jnp.zeros((EXTRA - 9, width), jnp.float32))
        out[0, half:, :] = jnp.concatenate(terms, axis=0).astype(jnp.bfloat16)

    return pl.pallas_call(
        kernel,
        grid=(count,),
        in_specs=[
            pl.BlockSpec((1, half, width), lambda i: (i, 1, 0)),
            pl.BlockSpec(stats.shape, lambda i: (0, 0)),
        ],
        out_specs=pl.BlockSpec((1, half + EXTRA, width), lambda i: (i, 0, 0)),
        out_shape=jax.ShapeDtypeStruct((count, half + EXTRA, width), quarters.dtype),
        compiler_params=settings(8),
        cost_estimate=FREE,
    )(quarters, stats)


def behind(value, *others):
    def kernel(*refs):
        pass

    return pl.pallas_call(
        kernel,
        in_specs=[ANYWHERE] * (1 + len(others)),
        out_specs=ANYWHERE,
        out_shape=jax.ShapeDtypeStruct(value.shape, value.dtype),
        input_output_aliases={0: 0},
        compiler_params=settings(1),
        cost_estimate=FREE,
    )(value, *others)


def carried(rows):
    rows = rows.astype(jnp.float32)
    return (rows[0:3] + rows[3:6]) + rows[6:9]


def standardized(piece, stats):
    piece = piece.astype(jnp.float32)
    return ((piece - stats[0:1, :]) * stats[1:2, :]).astype(jnp.bfloat16)


def own_product(place, dosages, stats):
    rows, width = dosages.shape
    half, chunk = width // 2, 1024

    def kernel(place, data, stats, kept, given, total, turned):
        step = pl.program_id(0)
        flat = standardized(data[...], stats)
        for start in range(0, chunk, 256):
            turned[:, start : start + 256] = flat[start : start + 256, :].T
        product = jnp.dot(turned[...], flat, preferred_element_type=jnp.float32)

        @pl.when(step == 0)
        def _():
            total[...] = product

        @pl.when(step > 0)
        def _():
            total[...] += product

        @pl.when(step == pl.num_programs(0) - 1)
        def _():
            core = place[1]
            kept[...] = total[pl.ds(pl.multiple_of(core * half, half), half), :]
            other = total[pl.ds(pl.multiple_of((1 - core) * half, half), half), :]
            given[...] = other.astype(jnp.bfloat16)

    fixed = lambda i: (0, 0)
    return pl.pallas_call(
        kernel,
        grid=(rows // chunk,),
        in_specs=[
            SCALARS,
            pl.BlockSpec((chunk, width), lambda i: (i, 0)),
            pl.BlockSpec(stats.shape, fixed),
        ],
        out_specs=[pl.BlockSpec((half, width), fixed)] * 2,
        out_shape=[
            jax.ShapeDtypeStruct((half, width), jnp.float32),
            jax.ShapeDtypeStruct((half, width), jnp.bfloat16),
        ],
        scratch_shapes=[
            pltpu.VMEM((width, width), jnp.float32),
            pltpu.VMEM((width, chunk), jnp.bfloat16),
        ],
        compiler_params=settings(20),
        cost_estimate=FREE,
    )(place, dosages, stats)


def prepared(place, first, second, after):
    count, depth, width = first.shape
    half = width // 2

    def kernel(place, first, second, *refs):
        out, kept, given, stats = refs[-4:]
        stats[0] = carried(second[0, depth:, :])
        out[0, :depth, :] = standardized(first[0], stats.at[0])
        out[0, depth:, :] = standardized(second[0, :depth, :], stats.at[0])
        core = place[1]
        kept[0] = out[0, :, pl.ds(pl.multiple_of(core * half, half), half)]
        given[0] = out[0, :, pl.ds(pl.multiple_of((1 - core) * half, half), half)]

    shapes = [(2 * count - 1, 2 * depth, width)] + [(count, 2 * depth, half)] * 2
    whole = lambda *shape: pl.BlockSpec((1, *shape), lambda i: (i, 0, 0))
    return pl.pallas_call(
        kernel,
        grid=(count,),
        in_specs=[SCALARS, whole(depth, width), whole(depth + EXTRA, width)]
        + [ANYWHERE] * len(after),
        out_specs=[whole(*shape[1:]) for shape in shapes] + [whole(3, width)],
        out_shape=[jax.ShapeDtypeStruct(shape, jnp.bfloat16) for shape in shapes]
        + [jax.ShapeDtypeStruct((count, 3, width), jnp.float32)],
        compiler_params=settings(20),
        cost_estimate=FREE,
    )(place, first, second, *after)


def prepared_ahead(first, second, blocks):
    count, depth, width = first.shape

    def kernel(first, second, blocks, out, stats):
        stats[0] = carried(second[0, depth:, :])
        out[0, :depth, :] = standardized(first[0], stats.at[0])
        out[0, depth:, :] = standardized(second[0, :depth, :], stats.at[0])

    whole = lambda *shape: pl.BlockSpec((1, *shape), lambda i: (i, 0, 0))
    return pl.pallas_call(
        kernel,
        grid=(count,),
        in_specs=[whole(depth, width), whole(depth + EXTRA, width), ANYWHERE],
        out_specs=[
            pl.BlockSpec((1, 2 * depth, width), lambda i: (RING + i, 0, 0)),
            whole(3, width),
        ],
        out_shape=[
            jax.ShapeDtypeStruct(blocks.shape, blocks.dtype),
            jax.ShapeDtypeStruct((count, 3, width), jnp.float32),
        ],
        input_output_aliases={2: 0},
        compiler_params=settings(20),
        cost_estimate=FREE,
    )(first, second, blocks)


def summed(own, parts, shared, after):
    half, width = own.shape
    count = len(parts)

    def kernel(own, *refs):
        parts, shared, out = refs[:count], refs[count], refs[-1]
        total = own[...]
        for part in parts:
            total = total + part[...].astype(jnp.float32)
        out[...] = (total - shared[...]).astype(jnp.bfloat16)

    return pl.pallas_call(
        kernel,
        in_specs=[WHOLE] * (count + 2) + [ANYWHERE] * len(after),
        out_shape=jax.ShapeDtypeStruct((half, width), jnp.bfloat16),
        compiler_params=settings(8),
        cost_estimate=FREE,
    )(own, *parts, shared, *after)


def assembled(place, mine, theirs):
    half, width = mine[0].shape
    count = len(mine)

    def kernel(place, *refs):
        out = refs[-1]
        core = place[1]
        for index in range(count):
            columns = slice(index * width, (index + 1) * width)
            out[pl.ds(pl.multiple_of(core * half, half), half), columns] = refs[index][...]
            out[pl.ds(pl.multiple_of((1 - core) * half, half), half), columns] = refs[
                count + index
            ][...]

    return pl.pallas_call(
        kernel,
        in_specs=[SCALARS] + [WHOLE] * (2 * count),
        out_shape=jax.ShapeDtypeStruct((2 * half, count * width), jnp.bfloat16),
        compiler_params=settings(8),
        cost_estimate=FREE,
    )(place, *mine, *theirs)


def per_device(dosages, window_end):
    rows, width = dosages.shape
    count = lax.axis_size("var")
    total = rows * lax.axis_size("samp")
    var, samp = lax.axis_index("var"), lax.axis_index("samp")
    x, core = var % RING, samp % 2
    half = width // 2
    place = jnp.stack([x, core]).astype(jnp.int32)

    core_pairs, far_pairs = to_core(count), to_far(count)
    rings = [list(range(first, first + RING)) for first in range(0, count, RING)]

    data = dosages.astype(jnp.float32)
    sums = jnp.stack([jnp.sum(data, axis=0), jnp.sum(data * data, axis=0)])
    sums = jnp.stack([sums, moved(sums, far_pairs)])
    sums, far_sums = sums + moved(sums, core_pairs)
    mean = (sums[0] + far_sums[0]) / total
    spread = 1.0 / jnp.sqrt((sums[1] + far_sums[1]) / total - mean * mean + 1e-05)
    tilt = (sums[0] - far_sums[0]) / total * spread * (total / 2) ** 0.5
    own_stats = jnp.stack([mean, spread, tilt])

    all_quarters = dosages.reshape(RING, rows // RING, width)

    def dealt(value):
        return lax.all_to_all(value, "var", 0, 0, axis_index_groups=rings)

    here = [dealt(all_quarters[:, : rows // RING // 2])]
    here.append(dealt(behind(with_statistics(all_quarters, own_stats), here[0])))
    back_pairs = to_ring_before(count)
    ahead = [moved(here[0][: RING - 1], back_pairs)]
    ahead.append(moved(behind(here[1][: RING - 1], ahead[0]), back_pairs))

    own_kept, own_given = own_product(place, dosages, own_stats)
    own = own_kept + moved(own_given, core_pairs).astype(jnp.float32)
    rising = lax.dynamic_slice_in_dim(tilt, core * half, half, 0)[:, None]
    values = [(own - rising * tilt[None, :]).astype(jnp.bfloat16)]
    blocks, kept_rows, given_rows, ring_stats = prepared(place, *here, values + ahead[:1])
    blocks, ahead_stats = prepared_ahead(*ahead, blocks)
    tilts = jnp.concatenate([ring_stats[:, 2], ahead_stats[:, 2]])

    ends = lax.dynamic_slice_in_dim(window_end, core * half, half, 0)
    columns = jnp.arange(width, dtype=jnp.int32)

    def shared(step):
        return rising * lax.dynamic_slice_in_dim(tilts, x + step, 1, 0)

    def finished(step, value, other):
        both = rising * tilt[None, :] if step == 0 else shared(step)
        gram = value.astype(jnp.float32) + other.astype(jnp.float32) + 2.0 * both
        if step:
            target = (var + step) * width + columns
            gram = jnp.where(target[None, :] <= ends[:, None], gram, 0.0)
        return (gram / total).astype(jnp.bfloat16)

    far = [moved(behind(values[0], ahead[1]), far_pairs)]
    mine = [finished(0, values[0], far[0])]
    theirs = [moved(mine[0], core_pairs)]
    for step in (1, 2, 3):
        if step > 1:
            given_rows = behind(given_rows, *sent)
        product = lambda left: jnp.einsum(
            "zsa,zsb->zab",
            left,
            blocks[step : step + RING],
            preferred_element_type=jnp.float32,
        )
        received = moved(product(given_rows).astype(jnp.bfloat16), core_pairs)
        kept = product(kept_rows)

        def part(d):
            at = lambda array: lax.dynamic_index_in_dim(array, (x + d) % RING, 0, False)
            return at(kept) + at(received).astype(jnp.float32)

        sent = [part(d).astype(jnp.bfloat16) for d in (1, 3, 2)]
        parts = [moved(one, along_ring(count, d)) for one, d in zip(sent, (1, 3, 2))]
        after = theirs[step - 2 : step - 1] if step > 1 else []
        values.append(summed(part(0), parts, shared(step), after))
        far.append(moved(values[step], far_pairs))
        mine.append(finished(step, values[step], far[step]))
        theirs.append(moved(mine[step], core_pairs))
    return assembled(place, mine, theirs)


def solution(mesh):
    placed = (P("samp", "var"), P("var"))
    return jax.shard_map(
        per_device, mesh=mesh, in_specs=placed, out_specs=P("var", None), check_vma=False
    )
```
